512 devices in a mesh: inst: 64 (over x, z), tp: 8 (over y, core).
Axes of the slice: x: 4, y: 4, z: 16, core: 2. Of those that a mesh axis runs over, the one named last changes fastest.
Arguments:
- queries: bfloat16 [256, 2, 4096], P('inst', None, 'tp'), may hold values from -120 to 120
- keys_new: bfloat16 [256, 2, 1024], P('inst', None, 'tp'), may hold values from -6 to 6
- values_new: bfloat16 [256, 2, 1024], P('inst', None, 'tp'), may hold values from -6 to 6
- key_cache: bfloat16 [192, 1024, 1024], P('inst', None, 'tp'), may hold values from -6 to 6
- value_cache: bfloat16 [192, 1024, 1024], P('inst', None, 'tp'), may hold values from -6 to 6
- lengths: int32 [192], replicated, may hold values from 128 to 1022, as said below
- migration: int32 [64, 2], replicated, may hold values from 0 to 63, as said below
- out_weight: bfloat16 [4096, 3072], P('tp'), may hold values from -1.5 to 1.5
Outputs:
- attended: bfloat16 [256, 2, 3072], P('inst', None, 'tp')
- key_out: bfloat16 [256, 1024, 1024], P('inst', None, 'tp')
- value_out: bfloat16 [256, 1024, 1024], P('inst', None, 'tp')
The draws below stay inside these ranges and needn't reach their ends.
Inputs may be any that keep to these rules, and one draw needn't show every extreme that they name: `lengths`: at least one request has length 1022. `migration`: column 0 is a resident slot below 3; column 1 holds every instance once.
All inputs are finite; a program needn't handle non-finite values.
Results may differ from the reference program's by a relative error of at most 0.012.
The reference program's roundings to bfloat16 on the way count: a program that leaves them out, or rounds other values in their place, can miss the bound.
Values may be sent and summed in bfloat16 or wider, within the bound.
A program may use at most 64 MiB of HBM per device.

```python
import jax
import jax.numpy as jnp
from jax import lax

D = 3072
QHEADS = 32
KV_HEADS = 8
HEAD_DIM = 128
STEPS = 2
RES = 3
MAXLEN = 1024
INSTANCES = 64
ROWS = 256
RES_ROWS = 192


def draw_queries(key, part):
    key = jax.random.fold_in(key, 11)
    first = jax.random.fold_in(key, 0)
    values_out = jnp.clip(1.5 * jax.random.normal(first, (ROWS, STEPS, QHEADS, HEAD_DIM), jnp.float32), -9.0, 9.0)
    return values_out.reshape(ROWS, STEPS, QHEADS * HEAD_DIM).astype(jnp.bfloat16)


def draw_lengths(key, part):
    key = jax.random.fold_in(key, 23)
    first, second = jax.random.split(key)
    drawn = jax.random.randint(first, (RES_ROWS,), MAXLEN // 8, MAXLEN - STEPS + 1, dtype=jnp.int32)
    place = jax.random.randint(second, (), 0, RES_ROWS, dtype=jnp.int32)
    return drawn.at[place].set(MAXLEN - STEPS).astype(jnp.int32)


def draw_migration(key, part):
    key = jax.random.fold_in(key, 37)
    first, second = jax.random.split(key)
    slots_out = jax.random.randint(first, (INSTANCES,), 0, RES, dtype=jnp.int32)
    targets = jax.random.permutation(second, INSTANCES).astype(jnp.int32)
    return jnp.stack([slots_out, targets], axis=1).astype(jnp.int32)


def block_scale(stream_key, extent, pieces, low, largest):
    loudness, own = 1.0, jax.random.fold_in(stream_key, 6)
    for position, parts in pieces:
        steps = jnp.exp(jax.random.uniform(jax.random.fold_in(own, position), (parts,), jnp.float32, low / len(pieces), largest / len(pieces)))
        loudness = loudness * jnp.repeat(steps, extent[position] // parts).reshape([-1 if axis == position else 1 for axis in range(len(extent))])
    return loudness


def scatter_about(stream_key, shape, scale, most, shards=(), kind=jnp.bfloat16):
    result = jax.random.normal(stream_key, shape, jnp.float32) * scale
    if len(shards) > 0:
        result = block_scale(stream_key, shape, shards, -0.22, 0.18) * result
    return jnp.clip(result, min=-most, max=most).astype(kind)


def setup_inputs(seed: int = 0) -> dict:
    splits = jax.random.split(jax.random.key(seed), 9)
    return {
        "queries": draw_queries(jax.random.fold_in(splits[8], 71), 0),
        "keys_new": scatter_about(splits[1], (ROWS, STEPS, KV_HEADS * HEAD_DIM), 1.0, 6.0, ((0, 64), (2, 8))),
        "values_new": scatter_about(splits[2], (ROWS, STEPS, KV_HEADS * HEAD_DIM), 1.0, 6.0, ((0, 64), (2, 8))),
        "key_cache": scatter_about(splits[3], (RES_ROWS, MAXLEN, KV_HEADS * HEAD_DIM), 1.0, 6.0, ((0, 64), (2, 8))),
        "value_cache": scatter_about(splits[4], (RES_ROWS, MAXLEN, KV_HEADS * HEAD_DIM), 1.0, 6.0, ((0, 64), (2, 8))),
        "lengths": draw_lengths(jax.random.fold_in(splits[8], 71), 0),
        "migration": draw_migration(jax.random.fold_in(splits[8], 71), 0),
        "out_weight": scatter_about(splits[7], (QHEADS * HEAD_DIM, D), 0.25, 1.5, ((0, 8),)),
    }


theta_base = 1000000.0


def rotate(values_in, positions):
    half_size = values_in.shape[-1] // 2
    frequency = jnp.exp(-jnp.log(theta_base) * 2.0 * jnp.arange(half_size, dtype=jnp.float32) / values_in.shape[-1])
    angles = positions[:, :, None, None] * frequency[None, None, None, :]
    cosine_part = jnp.concatenate([jnp.cos(angles), jnp.cos(angles)], axis=-1)
    sine_part = jnp.concatenate([jnp.sin(angles), jnp.sin(angles)], axis=-1)
    rotated = jnp.concatenate([-values_in[..., half_size:], values_in[..., :half_size]], axis=-1)
    return values_in * cosine_part + rotated * sine_part


def attend(query, key_new, value_new, key_cache, value_cache, length):
    batch_rows, step_count, query_width = query.shape
    kv_width = key_new.shape[-1]
    groups = kv_width // HEAD_DIM
    group_size = query_width // kv_width
    window = key_cache.shape[1]
    positions = (length[:, None] + jnp.arange(step_count, dtype=jnp.int32)[None, :]).astype(jnp.float32)
    query_rot = rotate(query.astype(jnp.float32).reshape(batch_rows, step_count, groups * group_size, HEAD_DIM), positions).astype(jnp.bfloat16)
    key_rot_low = rotate(key_new.astype(jnp.float32).reshape(batch_rows, step_count, groups, HEAD_DIM), positions).astype(jnp.bfloat16)
    query_rot = query_rot.reshape(batch_rows, step_count, groups, group_size, HEAD_DIM).astype(jnp.float32)
    key_rot = key_rot_low.astype(jnp.float32)
    cache_keys = key_cache.reshape(batch_rows, window, groups, HEAD_DIM).astype(jnp.float32)
    cache_values = value_cache.reshape(batch_rows, window, groups, HEAD_DIM).astype(jnp.float32)
    fresh_values = value_new.reshape(batch_rows, step_count, groups, HEAD_DIM).astype(jnp.float32)
    score_scale = HEAD_DIM ** -0.5
    cache_scores = jnp.einsum("stgrd,slgd->stgrl", query_rot, cache_keys) * score_scale
    new_scores = jnp.einsum("stgrd,sugd->stgru", query_rot, key_rot) * score_scale
    live_cache = jnp.arange(window, dtype=jnp.int32)[None, :] < length[:, None]
    live_new = jnp.arange(step_count)[None, :] <= jnp.arange(step_count)[:, None]
    cache_scores = jnp.where(live_cache[:, None, None, None, :], cache_scores, -1e30)
    new_scores = jnp.where(live_new[None, :, None, None, :], new_scores, -1e30)
    row_top = jnp.maximum(jnp.max(cache_scores, axis=-1), jnp.max(new_scores, axis=-1))[..., None]
    cache_exp = jnp.exp(cache_scores - row_top)
    new_exp = jnp.exp(new_scores - row_top)
    denominator = jnp.sum(cache_exp, axis=-1, keepdims=True) + jnp.sum(new_exp, axis=-1, keepdims=True)
    cache_probs = (cache_exp / denominator).astype(jnp.bfloat16).astype(jnp.float32)
    new_probs = (new_exp / denominator).astype(jnp.bfloat16).astype(jnp.float32)
    mixed = jnp.einsum("stgrl,slgd->stgrd", cache_probs, cache_values) + jnp.einsum("stgru,sugd->stgrd", new_probs, fresh_values)
    return mixed.reshape(batch_rows, step_count, query_width).astype(jnp.bfloat16), key_rot_low.reshape(batch_rows, step_count, kv_width)


def reference(queries, keys_new, values_new, key_cache, value_cache, lengths, migration, out_weight):
    instances = jnp.arange(INSTANCES, dtype=jnp.int32)
    slots_out = migration[:, 0].astype(jnp.int32)
    targets = migration[:, 1].astype(jnp.int32)
    anchor = jnp.sum(jnp.where(targets[:, None] == instances[None, :], instances[:, None], 0), axis=0).astype(jnp.int32)
    row_inst = jnp.repeat(instances, RES + 1)
    row_slot = jnp.tile(jnp.arange(RES + 1, dtype=jnp.int32), INSTANCES)
    source = anchor[row_inst]
    landing = row_slot == RES
    cache_row = jnp.where(landing, source * RES + slots_out[source], row_inst * RES + jnp.minimum(row_slot, RES - 1)).astype(jnp.int32)
    freed = jnp.logical_and(jnp.logical_not(landing), row_slot == slots_out[row_inst])
    context = jnp.where(freed, 0, lengths[cache_row]).astype(jnp.int32)
    zero_index = jnp.zeros((), jnp.int32)

    def one_row(packed):
        query, key_new, value_new, row_index, length = packed
        cache_keys = lax.dynamic_index_in_dim(key_cache, row_index, 0)
        cache_values = lax.dynamic_index_in_dim(value_cache, row_index, 0)
        mixed, key_rot = attend(query[None], key_new[None], value_new[None], cache_keys, cache_values, length[None])
        keys_written = lax.dynamic_update_slice(cache_keys[0], key_rot[0], (length.astype(jnp.int32), zero_index))
        values_written = lax.dynamic_update_slice(cache_values[0], value_new, (length.astype(jnp.int32), zero_index))
        return mixed[0], keys_written, values_written

    mixed, key_out, value_out = lax.map(one_row, (queries, keys_new, values_new, cache_row, context))
    flat_rows = mixed.reshape(-1, mixed.shape[-1])
    projected = jnp.dot(flat_rows, out_weight, preferred_element_type=jnp.float32)
    attended = projected.astype(jnp.bfloat16).reshape(queries.shape[0], queries.shape[1], out_weight.shape[1])
    return attended, key_out, value_out
```

```python
import functools

import jax
import jax.numpy as jnp
from jax import lax
from jax.experimental import pallas as pl
from jax.experimental.pallas import tpu as pltpu
from jax.sharding import PartitionSpec as P

MESH = pl.DeviceIdType.MESH
HEAD = 128
THETA = 1000000.0
XS, ZS = 4, 16
INST = XS * ZS
TP = 8
RES = 3
WINDOW = 1024
PIECE = WINDOW // INST
STEPS = 2
HEADS = 4
F32 = jnp.float32
BF16 = jnp.bfloat16


def peer(j, x, z):
    dx = 3 - lax.rem(j, 4)
    t = 15 - j // 4
    dz = lax.rem(jnp.where(lax.rem(t, 2) == 1, (t + 1) // 2, ZS - t // 2), ZS)
    return dx * ZS + dz, lax.rem(x + dx, XS) * ZS + lax.rem(z + dz, ZS)


def rows_of(i):
    return pl.ds(pl.multiple_of(i * PIECE, PIECE), PIECE)


def rotate(v, cos, sin):
    lane = lax.broadcasted_iota(jnp.int32, v.shape, 1)
    turned = pltpu.roll(v, HEAD // 2, 1)
    return v * cos + jnp.where(lane < HEAD // 2, -turned, turned) * sin


def kernel(
    lengths_h, mig_h, queries_h, keys_h, values_h, kc, vc, w,
    attended, ko, vo,
    lengths, mig, mig_v, queries, keys_new, values_new,
    res_k, res_v, arr, stage, spread_k, spread_v, ordered, wv, plan_v, plan,
    qr, kr, prob, fresh, mixed, part, got, part_l, got_l,
    i_sem, a_sem, s_sem, r_sem, o_sem, p_send, p_recv,
):
    res, spread = (res_k, res_v), (spread_k, spread_v)
    me = lax.axis_index("inst")
    tp = lax.axis_index("tp")
    x, z = me // ZS, lax.rem(me, ZS)

    barrier = pltpu.get_barrier_semaphore()

    def greet(j, _):
        _, d = peer(j, x, z)
        pl.semaphore_signal(barrier, inc=1, device_id={"inst": d}, device_id_type=MESH)
        return 0

    lax.fori_loop(0, INST - 1, greet, 0)

    def greet_tp(j, _):
        pl.semaphore_signal(barrier, inc=1, device_id={"tp": lax.rem(tp + j, TP)}, device_id_type=MESH)
        return 0

    lax.fori_loop(1, TP, greet_tp, 0)

    pairs = [
        (mig_h, mig), (kc, res_k), (vc, res_v), (mig_h, mig_v), (lengths_h, lengths),
        (queries_h, queries), (keys_h, keys_new), (values_h, values_new), (w, wv),
    ]
    loads = [pltpu.make_async_copy(src, dst, i_sem.at[i]) for i, (src, dst) in enumerate(pairs)]
    for load in loads:
        load.start()

    def send_first(c):
        def step(j, _):
            o, d = peer(j, x, z)
            pltpu.make_async_remote_copy(
                stage.at[c, rows_of(d)], spread[c].at[o], s_sem.at[0, c], r_sem.at[0, c],
                device_id={"inst": d}, device_id_type=MESH,
            ).start()
            return 0

        lax.fori_loop(0, INST - 1, step, 0)
        spread[c][0] = stage[c, rows_of(me)]

    def send_second(c):
        def pick(d, _):
            ordered[c, rows_of(d)] = spread[c][plan[d, 1]]
            return 0

        lax.fori_loop(0, INST, pick, 0)

        def step(j, _):
            _, d = peer(j, x, z)
            pltpu.make_async_remote_copy(
                ordered.at[c, rows_of(d)], arr.at[c, rows_of(me)], s_sem.at[1, c], r_sem.at[1, c],
                device_id={"inst": d}, device_id_type=MESH,
            ).start()
            return 0

        lax.fori_loop(0, INST - 1, step, 0)
        arr[c, rows_of(me)] = ordered[c, rows_of(me)]

    def wait_bytes(sem, buf):
        pltpu.make_async_copy(buf, buf, sem).wait()

    sent = pl.ds(0, (INST - 1) * PIECE)
    loads[0].wait()
    leaving = mig[0, me]
    for c in range(2):
        loads[1 + c].wait()
        stage[c] = res[c][leaving]
    pl.semaphore_wait(barrier, INST - 1 + TP - 1)
    for c in range(2):
        send_first(c)
    for load in loads[3:8]:
        load.wait()

    s_of = lax.broadcasted_iota(jnp.int32, (INST, INST), 1)
    d_of = lax.broadcasted_iota(jnp.int32, (INST, INST), 0)
    anchor = jnp.max(jnp.where(mig_v[1:2, :] == d_of, s_of, 0), axis=1, keepdims=True)
    slot = ((x - lax.shift_right_logical(anchor, 4)) & (XS - 1)) * ZS + ((z - anchor) & (ZS - 1))
    column = lax.broadcasted_iota(jnp.int32, plan_v.shape, 1)
    plan_v[...] = jnp.where(column == 0, anchor, slot)
    to_smem = pltpu.make_async_copy(plan_v, plan, a_sem)
    to_smem.start()
    to_smem.wait()

    source = plan[me, 0]
    ctx = [jnp.where(leaving == k, 0, lengths[me * RES + k]) for k in range(RES)]
    ctx.append(lengths[source * RES + mig[0, source]])
    n_q = (RES + 1) * HEADS * STEPS
    row = lax.broadcasted_iota(jnp.int32, (n_q, HEAD), 0)
    freq_at = lax.rem(lax.broadcasted_iota(jnp.int32, (n_q, HEAD), 1), HEAD // 2).astype(F32)
    freq = jnp.exp(-jnp.log(jnp.float32(THETA)) * 2.0 * freq_at / HEAD)
    per = HEADS * STEPS
    pos = lax.rem(row, STEPS)
    for r in range(RES + 1):
        pos = pos + jnp.where(row // per == r, ctx[r], 0)
    angle = pos.astype(F32) * freq
    cos, sin = jnp.cos(angle), jnp.sin(angle)
    heads = []
    for r in range(RES + 1):
        flat = queries[r].astype(F32)
        heads += [flat[:, h * HEAD : (h + 1) * HEAD] for h in range(HEADS)]
    qr[...] = rotate(jnp.concatenate(heads, axis=0), cos, sin).astype(BF16).astype(F32)
    k_flat = jnp.concatenate([keys_new[r].astype(F32) for r in range(RES + 1)], axis=0)
    k_cos = jnp.concatenate([cos[r * per : r * per + STEPS] for r in range(RES + 1)], axis=0)
    k_sin = jnp.concatenate([sin[r * per : r * per + STEPS] for r in range(RES + 1)], axis=0)
    kr[...] = rotate(k_flat, k_cos, k_sin).astype(BF16).astype(F32)

    def write_tokens(r, c, buf):
        both = values_new[r].astype(F32) if c else kr[pl.ds(r * STEPS, STEPS), :]
        block = 128

        def step(i, _):
            at = pl.ds(pl.multiple_of(i * block, block), block)
            place = lax.broadcasted_iota(jnp.int32, (block, HEAD), 0) + i * block - ctx[r]
            old = buf[at, :].astype(F32)
            buf[at, :] = jnp.where(place == 0, both[0:1], jnp.where(place == 1, both[1:2], old)).astype(BF16)
            return 0

        lax.fori_loop(0, WINDOW // block, step, 0)
        pltpu.make_async_copy(buf, (ko, vo)[c].at[r], o_sem.at[c, r]).start()

    def weigh(r, keys):
        q = qr[pl.ds(r * per, per), :].astype(BF16)
        s = lax.dot_general(q, keys[...], (((1,), (1,)), ((), ())), preferred_element_type=F32)
        s = s * (HEAD**-0.5)
        place = lax.broadcasted_iota(jnp.int32, s.shape, 1) - ctx[r]
        step = lax.rem(lax.broadcasted_iota(jnp.int32, s.shape, 0), STEPS)
        s = jnp.where(place <= step, s, -1e30)
        e = jnp.exp(s - jnp.max(s, axis=1, keepdims=True))
        p = (e / jnp.sum(e, axis=1, keepdims=True)).astype(BF16).astype(F32)
        prob[r] = jnp.where(place < 0, p, 0.0)
        for t in range(STEPS):
            fresh[t] = jnp.broadcast_to(jnp.sum(jnp.where(place == t, p, 0.0), axis=1, keepdims=True), fresh.shape[1:])

    def mix(r, values, at):
        o = jnp.dot(prob[r].astype(BF16), values[...], preferred_element_type=F32)
        both = values_new[r].astype(F32)
        for t in range(STEPS):
            o = o + fresh[t] * both[t : t + 1]
        for h in range(HEADS):
            mixed[pl.ds(at, STEPS), pl.ds(h * HEAD, HEAD)] = o[h * STEPS : (h + 1) * STEPS]

    share = attended.shape[2]

    def scatter(terms, sums, n, k):
        out = jnp.dot(mixed[...].astype(BF16), wv[...], preferred_element_type=F32)
        for to in range(TP):
            terms[to] = out[:n, to * share : (to + 1) * share]
        copies = []
        for i in range(1, TP):
            to = lax.rem(tp + i, TP)
            copy = pltpu.make_async_remote_copy(
                terms.at[to], sums.at[i], p_send.at[k, i], p_recv.at[k, i],
                device_id={"tp": to}, device_id_type=MESH,
            )
            copy.start()
            copies.append(copy)
        sums[0] = terms[tp]
        return copies

    mixed[...] = jnp.zeros_like(mixed)
    for r in range(RES):
        write_tokens(r, 0, res_k.at[r])
        weigh(r, res_k.at[r])
        mix(r, res_v.at[r], r * STEPS)
        write_tokens(r, 1, res_v.at[r])

    wait_bytes(r_sem.at[0, 0], spread_k.at[pl.ds(1, INST - 1)])
    send_second(0)
    loads[8].wait()
    copies = scatter(part, got, RES * STEPS, 0)
    wait_bytes(r_sem.at[0, 1], spread_v.at[pl.ds(1, INST - 1)])
    send_second(1)
    for copy in copies:
        copy.wait()
    total = jnp.sum(got[...], axis=0)
    for r in range(RES):
        attended[r] = total[r * STEPS : (r + 1) * STEPS].astype(attended.dtype)

    wait_bytes(r_sem.at[1, 0], arr.at[0, sent])
    write_tokens(RES, 0, arr.at[0])
    weigh(RES, arr.at[0])
    for c in range(2):
        wait_bytes(s_sem.at[0, c], arr.at[c, sent])
    wait_bytes(s_sem.at[1, 0], arr.at[0, sent])
    for c in range(2):
        for r in range(RES + 1 - c):
            pltpu.make_async_copy(res_k.at[0], (ko, vo)[c].at[r], o_sem.at[c, r]).wait()

    wait_bytes(r_sem.at[1, 1], arr.at[1, sent])
    mix(RES, arr.at[1], 0)
    copies = scatter(part_l, got_l, STEPS, 1)
    write_tokens(RES, 1, arr.at[1])
    wait_bytes(s_sem.at[1, 1], arr.at[1, sent])
    pltpu.make_async_copy(arr.at[1], vo.at[RES], o_sem.at[1, RES]).wait()
    for copy in copies:
        copy.wait()
    attended[RES] = jnp.sum(got_l[...], axis=0).astype(attended.dtype)


def put(*refs):
    n = len(refs) // 2
    copies = [pltpu.make_async_copy(refs[i], refs[n + i], refs[-1].at[i]) for i in range(n)]
    for copy in copies:
        copy.start()
    for copy in copies:
        copy.wait()


def local(queries, keys_new, values_new, key_cache, value_cache, lengths, migration, out_weight):
    rows = queries.shape[0]
    share = out_weight.shape[1] // TP
    hbm, vmem, anywhere = (pl.BlockSpec(memory_space=m) for m in (pltpu.HBM, pltpu.VMEM, pl.ANY))
    cache = (WINDOW, HEAD)
    n_q = rows * HEADS * STEPS
    migration = migration.T
    shapes = [((rows, STEPS, share), BF16), ((rows, *cache), BF16), ((rows, *cache), BF16)]
    outs = pl.pallas_call(
        kernel,
        out_shape=[pltpu.VMEM(*s) for s in shapes],
        in_specs=[hbm] * 8,
        out_specs=[vmem, anywhere, anywhere],
        scratch_shapes=[
            pltpu.SMEM(lengths.shape, jnp.int32),
            pltpu.SMEM(migration.shape, jnp.int32),
            pltpu.VMEM(migration.shape, jnp.int32),
            pltpu.VMEM(queries.shape, BF16),
            pltpu.VMEM(keys_new.shape, BF16),
            pltpu.VMEM(values_new.shape, BF16),
            pltpu.VMEM((RES, *cache), BF16),
            pltpu.VMEM((RES, *cache), BF16),
            pltpu.VMEM((2, *cache), BF16),
            pltpu.VMEM((2, *cache), BF16),
            pltpu.VMEM((INST, PIECE, HEAD), BF16),
            pltpu.VMEM((INST, PIECE, HEAD), BF16),
            pltpu.VMEM((2, *cache), BF16),
            pltpu.VMEM(out_weight.shape, BF16),
            pltpu.VMEM((INST, 128), jnp.int32),
            pltpu.SMEM((INST, 128), jnp.int32),
            pltpu.VMEM((n_q, HEAD), F32),
            pltpu.VMEM((rows * STEPS, HEAD), F32),
            pltpu.VMEM((rows, HEADS * STEPS, WINDOW), F32),
            pltpu.VMEM((STEPS, HEADS * STEPS, HEAD), F32),
            pltpu.VMEM((8, HEADS * HEAD), F32),
            pltpu.VMEM((TP, RES * STEPS, share), F32),
            pltpu.VMEM((TP, RES * STEPS, share), F32),
            pltpu.VMEM((TP, STEPS, share), F32),
            pltpu.VMEM((TP, STEPS, share), F32),
            pltpu.SemaphoreType.DMA((9,)),
            pltpu.SemaphoreType.DMA,
            pltpu.SemaphoreType.DMA((2, 2)),
            pltpu.SemaphoreType.DMA((2, 2)),
            pltpu.SemaphoreType.DMA((2, rows)),
            pltpu.SemaphoreType.DMA((2, TP)),
            pltpu.SemaphoreType.DMA((2, TP)),
        ],
        compiler_params=pltpu.CompilerParams(
            collective_id=0, has_side_effects=True, vmem_limit_bytes=24 << 20
        ),
        cost_estimate=pl.CostEstimate(flops=50_000_000, bytes_accessed=8 << 20, transcendentals=40_000),
    )(*(
        pltpu.with_memory_space_constraint(v, pltpu.HBM)
        for v in (lengths, migration, queries, keys_new, values_new, key_cache, value_cache, out_weight)
    ))
    return pl.pallas_call(
        put,
        out_shape=[jax.ShapeDtypeStruct(*s) for s in shapes],
        in_specs=[anywhere] * 3,
        out_specs=[anywhere] * 3,
        scratch_shapes=[pltpu.SemaphoreType.DMA((3,))],
        compiler_params=pltpu.CompilerParams(vmem_limit_bytes=1 << 20),
        cost_estimate=pl.CostEstimate(flops=0, bytes_accessed=4 << 20, transcendentals=0),
    )(*(pltpu.with_memory_space_constraint(v, pltpu.VMEM) for v in outs))


def solution(mesh):
    in_specs = (
        P("inst", None, "tp"),
        P("inst", None, "tp"),
        P("inst", None, "tp"),
        P("inst", None, "tp"),
        P("inst", None, "tp"),
        P(),
        P(),
        P("tp", None),
    )
    out_specs = (P("inst", None, "tp"), P("inst", None, "tp"), P("inst", None, "tp"))
    return jax.shard_map(local, mesh=mesh, in_specs=in_specs, out_specs=out_specs, check_vma=False)
```

```python
import functools

import jax
import jax.numpy as jnp
from jax import lax
from jax.experimental import pallas as pl
from jax.experimental.pallas import tpu as pltpu
from jax.sharding import PartitionSpec as P

MESH = pl.DeviceIdType.MESH
HEAD = 128
THETA = 1000000.0
XS, ZS = 4, 16
INST = XS * ZS
TP = 8
RES = 3
WINDOW = 1024
PIECE = WINDOW // INST
STEPS = 2
FIRST = (0, 2, 4, 16)
HEADS = 4
F32 = jnp.float32
BF16 = jnp.bfloat16


def peer(j, x, z):
    dx = 3 - lax.rem(j, 4)
    t = 15 - j // 4
    dz = lax.rem(jnp.where(lax.rem(t, 2) == 1, (t + 1) // 2, ZS - t // 2), ZS)
    return dx * ZS + dz, lax.rem(x + dx, XS) * ZS + lax.rem(z + dz, ZS)


def rows_of(i):
    return pl.ds(pl.multiple_of(i * PIECE, PIECE), PIECE)


def rotate(v, cos, sin):
    lane = lax.broadcasted_iota(jnp.int32, v.shape, 1)
    turned = pltpu.roll(v, HEAD // 2, 1)
    return v * cos + jnp.where(lane < HEAD // 2, -turned, turned) * sin


def kernel(
    lengths_h, mig_h, queries_h, keys_h, values_h, kc, vc, w,
    attended, ko, vo,
    lengths, mig, mig_v, queries, keys_new, values_new,
    res_k, res_v, arr, stage, spread_k, spread_v, ordered, wv, plan_v, plan,
    qr, kr, prob, fresh, mixed, part, got, part_l, got_l,
    i_sem, a_sem, s_sem, r_sem, o_sem, p_send, p_recv,
):
    res, spread = (res_k, res_v), (spread_k, spread_v)
    me = lax.axis_index("inst")
    tp = lax.axis_index("tp")
    x, z = me // ZS, lax.rem(me, ZS)

    barrier = pltpu.get_barrier_semaphore()

    def greet(j, _):
        _, d = peer(j, x, z)
        pl.semaphore_signal(barrier, inc=1, device_id={"inst": d}, device_id_type=MESH)
        return 0

    lax.fori_loop(0, INST - 1, greet, 0)

    def greet_tp(j, _):
        pl.semaphore_signal(barrier, inc=1, device_id={"tp": lax.rem(tp + j, TP)}, device_id_type=MESH)
        return 0

    lax.fori_loop(1, TP, greet_tp, 0)

    pairs = [
        (mig_h, mig), (kc, res_k), (vc, res_v), (mig_h, mig_v), (lengths_h, lengths),
        (queries_h, queries), (keys_h, keys_new), (values_h, values_new), (w, wv),
    ]
    loads = [pltpu.make_async_copy(src, dst, i_sem.at[i]) for i, (src, dst) in enumerate(pairs)]
    for load in loads:
        load.start()

    def send_first(c):
        def step(j, _):
            o, d = peer(j, x, z)
            pltpu.make_async_remote_copy(
                stage.at[c, rows_of(d)], spread[c].at[o], s_sem.at[0, c], r_sem.at[0, c],
                device_id={"inst": d}, device_id_type=MESH,
            ).start()
            return 0

        lax.fori_loop(0, INST - 1, step, 0)
        spread[c][0] = stage[c, rows_of(me)]

    def send_second(c):
        def pick(d, _):
            ordered[c, rows_of(d)] = spread[c][plan[d, 1]]
            return 0

        lax.fori_loop(0, INST, pick, 0)

        def step(low, high, j, _):
            _, d = peer(j, x, z)
            zd = lax.rem(d, ZS)

            @pl.when(jnp.logical_and(zd >= low, zd < high))
            def _():
                pltpu.make_async_remote_copy(
                    ordered.at[c, rows_of(d)], arr.at[c, rows_of(me)], s_sem.at[1, c], r_sem.at[1, c],
                    device_id={"inst": d}, device_id_type=MESH,
                ).start()

            return 0

        for low, high in zip(FIRST, FIRST[1:]):
            lax.fori_loop(0, INST - 1, functools.partial(step, low, high), 0)
        arr[c, rows_of(me)] = ordered[c, rows_of(me)]

    def wait_bytes(sem, buf):
        pltpu.make_async_copy(buf, buf, sem).wait()

    sent = pl.ds(0, (INST - 1) * PIECE)
    loads[0].wait()
    leaving = mig[0, me]
    for c in range(2):
        loads[1 + c].wait()
        stage[c] = res[c][leaving]
    pl.semaphore_wait(barrier, INST - 1 + TP - 1)
    for c in range(2):
        send_first(c)
    for load in loads[3:8]:
        load.wait()

    s_of = lax.broadcasted_iota(jnp.int32, (INST, INST), 1)
    d_of = lax.broadcasted_iota(jnp.int32, (INST, INST), 0)
    anchor = jnp.max(jnp.where(mig_v[1:2, :] == d_of, s_of, 0), axis=1, keepdims=True)
    slot = ((x - lax.shift_right_logical(anchor, 4)) & (XS - 1)) * ZS + ((z - anchor) & (ZS - 1))
    column = lax.broadcasted_iota(jnp.int32, plan_v.shape, 1)
    plan_v[...] = jnp.where(column == 0, anchor, slot)
    to_smem = pltpu.make_async_copy(plan_v, plan, a_sem)
    to_smem.start()
    to_smem.wait()

    source = plan[me, 0]
    ctx = [jnp.where(leaving == k, 0, lengths[me * RES + k]) for k in range(RES)]
    ctx.append(lengths[source * RES + mig[0, source]])
    n_q = (RES + 1) * HEADS * STEPS
    row = lax.broadcasted_iota(jnp.int32, (n_q, HEAD), 0)
    freq_at = lax.rem(lax.broadcasted_iota(jnp.int32, (n_q, HEAD), 1), HEAD // 2).astype(F32)
    freq = jnp.exp(-jnp.log(jnp.float32(THETA)) * 2.0 * freq_at / HEAD)
    per = HEADS * STEPS
    pos = lax.rem(row, STEPS)
    for r in range(RES + 1):
        pos = pos + jnp.where(row // per == r, ctx[r], 0)
    angle = pos.astype(F32) * freq
    cos, sin = jnp.cos(angle), jnp.sin(angle)
    heads = []
    for r in range(RES + 1):
        flat = queries[r].astype(F32)
        heads += [flat[:, h * HEAD : (h + 1) * HEAD] for h in range(HEADS)]
    qr[...] = rotate(jnp.concatenate(heads, axis=0), cos, sin).astype(BF16).astype(F32)
    k_flat = jnp.concatenate([keys_new[r].astype(F32) for r in range(RES + 1)], axis=0)
    k_cos = jnp.concatenate([cos[r * per : r * per + STEPS] for r in range(RES + 1)], axis=0)
    k_sin = jnp.concatenate([sin[r * per : r * per + STEPS] for r in range(RES + 1)], axis=0)
    kr[...] = rotate(k_flat, k_cos, k_sin).astype(BF16).astype(F32)

    def write_tokens(r, c, buf):
        both = values_new[r].astype(F32) if c else kr[pl.ds(r * STEPS, STEPS), :]
        block = 128

        def step(i, _):
            at = pl.ds(pl.multiple_of(i * block, block), block)
            place = lax.broadcasted_iota(jnp.int32, (block, HEAD), 0) + i * block - ctx[r]
            old = buf[at, :].astype(F32)
            buf[at, :] = jnp.where(place == 0, both[0:1], jnp.where(place == 1, both[1:2], old)).astype(BF16)
            return 0

        lax.fori_loop(0, WINDOW // block, step, 0)
        pltpu.make_async_copy(buf, (ko, vo)[c].at[r], o_sem.at[c, r]).start()

    def weigh(r, keys):
        q = qr[pl.ds(r * per, per), :].astype(BF16)
        s = lax.dot_general(q, keys[...], (((1,), (1,)), ((), ())), preferred_element_type=F32)
        s = s * (HEAD**-0.5)
        place = lax.broadcasted_iota(jnp.int32, s.shape, 1) - ctx[r]
        step = lax.rem(lax.broadcasted_iota(jnp.int32, s.shape, 0), STEPS)
        s = jnp.where(place <= step, s, -1e30)
        e = jnp.exp(s - jnp.max(s, axis=1, keepdims=True))
        p = (e / jnp.sum(e, axis=1, keepdims=True)).astype(BF16).astype(F32)
        prob[r] = jnp.where(place < 0, p, 0.0)
        for t in range(STEPS):
            fresh[t] = jnp.broadcast_to(jnp.sum(jnp.where(place == t, p, 0.0), axis=1, keepdims=True), fresh.shape[1:])

    def mix(r, values, at):
        o = jnp.dot(prob[r].astype(BF16), values[...], preferred_element_type=F32)
        both = values_new[r].astype(F32)
        for t in range(STEPS):
            o = o + fresh[t] * both[t : t + 1]
        for h in range(HEADS):
            mixed[pl.ds(at, STEPS), pl.ds(h * HEAD, HEAD)] = o[h * STEPS : (h + 1) * STEPS]

    share = attended.shape[2]

    def scatter(terms, sums, n, k):
        out = jnp.dot(mixed[...].astype(BF16), wv[...], preferred_element_type=F32)
        for to in range(TP):
            terms[to] = out[:n, to * share : (to + 1) * share]
        for i in (4, 3, 5, 2, 6, 1, 7):
            to = lax.rem(tp + i, TP)
            pltpu.make_async_remote_copy(
                terms.at[to], sums.at[i], p_send.at[k], p_recv.at[k], device_id={"tp": to}, device_id_type=MESH
            ).start()
        sums[0] = terms[tp]

    mixed[...] = jnp.zeros_like(mixed)
    for r in range(RES):
        write_tokens(r, 0, res_k.at[r])
        weigh(r, res_k.at[r])
        mix(r, res_v.at[r], r * STEPS)
        write_tokens(r, 1, res_v.at[r])

    wait_bytes(r_sem.at[0, 0], spread_k.at[pl.ds(1, INST - 1)])
    send_second(0)
    loads[8].wait()
    scatter(part, got, RES * STEPS, 0)
    wait_bytes(r_sem.at[0, 1], spread_v.at[pl.ds(1, INST - 1)])
    send_second(1)
    others = pl.ds(1, TP - 1)
    wait_bytes(p_recv.at[0], got.at[others])
    total = jnp.sum(got[...], axis=0)
    for r in range(RES):
        attended[r] = total[r * STEPS : (r + 1) * STEPS].astype(attended.dtype)

    wait_bytes(r_sem.at[1, 0], arr.at[0, sent])
    write_tokens(RES, 0, arr.at[0])
    weigh(RES, arr.at[0])
    for c in range(2):
        wait_bytes(s_sem.at[0, c], arr.at[c, sent])
    wait_bytes(s_sem.at[1, 0], arr.at[0, sent])
    for c in range(2):
        for r in range(RES + 1 - c):
            pltpu.make_async_copy(res_k.at[0], (ko, vo)[c].at[r], o_sem.at[c, r]).wait()

    wait_bytes(r_sem.at[1, 1], arr.at[1, sent])
    mix(RES, arr.at[1], 0)
    scatter(part_l, got_l, STEPS, 1)
    write_tokens(RES, 1, arr.at[1])
    wait_bytes(p_send.at[0], part.at[others])
    wait_bytes(p_recv.at[1], got_l.at[others])
    attended[RES] = jnp.sum(got_l[...], axis=0).astype(attended.dtype)
    pltpu.make_async_copy(arr.at[1], vo.at[RES], o_sem.at[1, RES]).wait()
    wait_bytes(s_sem.at[1, 1], arr.at[1, sent])
    wait_bytes(p_send.at[1], part_l.at[others])


def put(*refs):
    n = len(refs) // 2
    copies = [pltpu.make_async_copy(refs[i], refs[n + i], refs[-1].at[i]) for i in range(n)]
    for copy in copies:
        copy.start()
    for copy in copies:
        copy.wait()


def local(queries, keys_new, values_new, key_cache, value_cache, lengths, migration, out_weight):
    rows = queries.shape[0]
    share = out_weight.shape[1] // TP
    hbm, vmem, anywhere = (pl.BlockSpec(memory_space=m) for m in (pltpu.HBM, pltpu.VMEM, pl.ANY))
    cache = (WINDOW, HEAD)
    n_q = rows * HEADS * STEPS
    migration = migration.T
    shapes = [((rows, STEPS, share), BF16), ((rows, *cache), BF16), ((rows, *cache), BF16)]
    outs = pl.pallas_call(
        kernel,
        out_shape=[pltpu.VMEM(*s) for s in shapes],
        in_specs=[hbm] * 8,
        out_specs=[vmem, anywhere, anywhere],
        scratch_shapes=[
            pltpu.SMEM(lengths.shape, jnp.int32),
            pltpu.SMEM(migration.shape, jnp.int32),
            pltpu.VMEM(migration.shape, jnp.int32),
            pltpu.VMEM(queries.shape, BF16),
            pltpu.VMEM(keys_new.shape, BF16),
            pltpu.VMEM(values_new.shape, BF16),
            pltpu.VMEM((RES, *cache), BF16),
            pltpu.VMEM((RES, *cache), BF16),
            pltpu.VMEM((2, *cache), BF16),
            pltpu.VMEM((2, *cache), BF16),
            pltpu.VMEM((INST, PIECE, HEAD), BF16),
            pltpu.VMEM((INST, PIECE, HEAD), BF16),
            pltpu.VMEM((2, *cache), BF16),
            pltpu.VMEM(out_weight.shape, BF16),
            pltpu.VMEM((INST, 128), jnp.int32),
            pltpu.SMEM((INST, 128), jnp.int32),
            pltpu.VMEM((n_q, HEAD), F32),
            pltpu.VMEM((rows * STEPS, HEAD), F32),
            pltpu.VMEM((rows, HEADS * STEPS, WINDOW), F32),
            pltpu.VMEM((STEPS, HEADS * STEPS, HEAD), F32),
            pltpu.VMEM((8, HEADS * HEAD), F32),
            pltpu.VMEM((TP, RES * STEPS, share), F32),
            pltpu.VMEM((TP, RES * STEPS, share), F32),
            pltpu.VMEM((TP, STEPS, share), F32),
            pltpu.VMEM((TP, STEPS, share), F32),
            pltpu.SemaphoreType.DMA((9,)),
            pltpu.SemaphoreType.DMA,
            pltpu.SemaphoreType.DMA((2, 2)),
            pltpu.SemaphoreType.DMA((2, 2)),
            pltpu.SemaphoreType.DMA((2, rows)),
            pltpu.SemaphoreType.DMA((2,)),
            pltpu.SemaphoreType.DMA((2,)),
        ],
        compiler_params=pltpu.CompilerParams(
            collective_id=0, has_side_effects=True, vmem_limit_bytes=24 << 20
        ),
        cost_estimate=pl.CostEstimate(flops=50_000_000, bytes_accessed=8 << 20, transcendentals=40_000),
    )(*(
        pltpu.with_memory_space_constraint(v, pltpu.HBM)
        for v in (lengths, migration, queries, keys_new, values_new, key_cache, value_cache, out_weight)
    ))
    return pl.pallas_call(
        put,
        out_shape=[jax.ShapeDtypeStruct(*s) for s in shapes],
        in_specs=[anywhere] * 3,
        out_specs=[anywhere] * 3,
        scratch_shapes=[pltpu.SemaphoreType.DMA((3,))],
        compiler_params=pltpu.CompilerParams(vmem_limit_bytes=1 << 20),
        cost_estimate=pl.CostEstimate(flops=0, bytes_accessed=4 << 20, transcendentals=0),
    )(*(pltpu.with_memory_space_constraint(v, pltpu.VMEM) for v in outs))


def solution(mesh):
    in_specs = (
        P("inst", None, "tp"),
        P("inst", None, "tp"),
        P("inst", None, "tp"),
        P("inst", None, "tp"),
        P("inst", None, "tp"),
        P(),
        P(),
        P("tp", None),
    )
    out_specs = (P("inst", None, "tp"), P("inst", None, "tp"), P("inst", None, "tp"))
    return jax.shard_map(local, mesh=mesh, in_specs=in_specs, out_specs=out_specs, check_vma=False)
```

```python
import functools

import jax
import jax.numpy as jnp
from jax import lax
from jax.experimental import pallas as pl
from jax.experimental.pallas import tpu as pltpu
from jax.sharding import PartitionSpec as P

MESH = pl.DeviceIdType.MESH
HEAD = 128
THETA = 1000000.0
XS, ZS = 4, 16
INST = XS * ZS
TP = 8
RES = 3
WINDOW = 1024
PIECE = WINDOW // INST
STEPS = 2
FIRST = (0, 2, 4, 16)
HEADS = 4
F32 = jnp.float32
BF16 = jnp.bfloat16


def peer(j, x, z):
    dx = 3 - lax.rem(j, 4)
    t = 15 - j // 4
    dz = lax.rem(jnp.where(lax.rem(t, 2) == 1, (t + 1) // 2, ZS - t // 2), ZS)
    return dx * ZS + dz, lax.rem(x + dx, XS) * ZS + lax.rem(z + dz, ZS)


def rows_of(i):
    return pl.ds(pl.multiple_of(i * PIECE, PIECE), PIECE)


def rotate(v, cos, sin):
    lane = lax.broadcasted_iota(jnp.int32, v.shape, 1)
    turned = pltpu.roll(v, HEAD // 2, 1)
    return v * cos + jnp.where(lane < HEAD // 2, -turned, turned) * sin


def kernel(
    lengths_h, mig_h, queries_h, keys_h, values_h, kc, vc, w,
    attended, ko, vo,
    lengths, mig, mig_v, queries, keys_new, values_new,
    res_k, res_v, arr, stage, spread_k, spread_v, ordered, wv, plan_v, plan,
    qr, kr, prob, fresh, mixed, part, got, part_l, got_l,
    i_sem, a_sem, s_sem, r_sem, o_sem, p_send, p_recv,
):
    res, spread = (res_k, res_v), (spread_k, spread_v)
    me = lax.axis_index("inst")
    tp = lax.axis_index("tp")
    x, z = me // ZS, lax.rem(me, ZS)

    barrier = pltpu.get_barrier_semaphore()

    def greet(j, _):
        _, d = peer(j, x, z)
        pl.semaphore_signal(barrier, inc=1, device_id={"inst": d}, device_id_type=MESH)
        return 0

    lax.fori_loop(0, INST - 1, greet, 0)

    def greet_tp(j, _):
        pl.semaphore_signal(barrier, inc=1, device_id={"tp": lax.rem(tp + j, TP)}, device_id_type=MESH)
        return 0

    lax.fori_loop(1, TP, greet_tp, 0)

    pairs = [
        (mig_h, mig), (kc, res_k), (vc, res_v), (mig_h, mig_v), (lengths_h, lengths),
        (queries_h, queries), (keys_h, keys_new), (values_h, values_new), (w, wv),
    ]
    loads = [pltpu.make_async_copy(src, dst, i_sem.at[i]) for i, (src, dst) in enumerate(pairs)]
    for load in loads:
        load.start()

    def send_first(c):
        def step(j, _):
            o, d = peer(j, x, z)
            pltpu.make_async_remote_copy(
                stage.at[c, rows_of(d)], spread[c].at[o], s_sem.at[0, c], r_sem.at[0, c],
                device_id={"inst": d}, device_id_type=MESH,
            ).start()
            return 0

        lax.fori_loop(0, INST - 1, step, 0)
        spread[c][0] = stage[c, rows_of(me)]

    def send_second(c):
        def pick(d, _):
            ordered[c, rows_of(d)] = spread[c][plan[d, 1]]
            return 0

        lax.fori_loop(0, INST, pick, 0)

        def step(low, high, j, _):
            _, d = peer(j, x, z)
            zd = lax.rem(d, ZS)

            @pl.when(jnp.logical_and(zd >= low, zd < high))
            def _():
                pltpu.make_async_remote_copy(
                    ordered.at[c, rows_of(d)], arr.at[c, rows_of(me)], s_sem.at[1, c], r_sem.at[1, c],
                    device_id={"inst": d}, device_id_type=MESH,
                ).start()

            return 0

        for low, high in zip(FIRST, FIRST[1:]):
            lax.fori_loop(0, INST - 1, functools.partial(step, low, high), 0)
        arr[c, rows_of(me)] = ordered[c, rows_of(me)]

    def wait_bytes(sem, buf):
        pltpu.make_async_copy(buf, buf, sem).wait()

    sent = pl.ds(0, (INST - 1) * PIECE)
    loads[0].wait()
    leaving = mig[0, me]
    for c in range(2):
        loads[1 + c].wait()
        stage[c] = res[c][leaving]
    pl.semaphore_wait(barrier, INST - 1 + TP - 1)
    for c in range(2):
        send_first(c)
    for load in loads[3:8]:
        load.wait()

    s_of = lax.broadcasted_iota(jnp.int32, (INST, INST), 1)
    d_of = lax.broadcasted_iota(jnp.int32, (INST, INST), 0)
    anchor = jnp.max(jnp.where(mig_v[1:2, :] == d_of, s_of, 0), axis=1, keepdims=True)
    slot = ((x - lax.shift_right_logical(anchor, 4)) & (XS - 1)) * ZS + ((z - anchor) & (ZS - 1))
    column = lax.broadcasted_iota(jnp.int32, plan_v.shape, 1)
    plan_v[...] = jnp.where(column == 0, anchor, slot)
    to_smem = pltpu.make_async_copy(plan_v, plan, a_sem)
    to_smem.start()
    to_smem.wait()

    source = plan[me, 0]
    ctx = [jnp.where(leaving == k, 0, lengths[me * RES + k]) for k in range(RES)]
    ctx.append(lengths[source * RES + mig[0, source]])
    n_q = (RES + 1) * HEADS * STEPS
    row = lax.broadcasted_iota(jnp.int32, (n_q, HEAD), 0)
    freq_at = lax.rem(lax.broadcasted_iota(jnp.int32, (n_q, HEAD), 1), HEAD // 2).astype(F32)
    freq = jnp.exp(-jnp.log(jnp.float32(THETA)) * 2.0 * freq_at / HEAD)
    per = HEADS * STEPS
    pos = lax.rem(row, STEPS)
    for r in range(RES + 1):
        pos = pos + jnp.where(row // per == r, ctx[r], 0)
    angle = pos.astype(F32) * freq
    cos, sin = jnp.cos(angle), jnp.sin(angle)
    heads = []
    for r in range(RES + 1):
        flat = queries[r].astype(F32)
        heads += [flat[:, h * HEAD : (h + 1) * HEAD] for h in range(HEADS)]
    qr[...] = rotate(jnp.concatenate(heads, axis=0), cos, sin).astype(BF16).astype(F32)
    k_flat = jnp.concatenate([keys_new[r].astype(F32) for r in range(RES + 1)], axis=0)
    k_cos = jnp.concatenate([cos[r * per : r * per + STEPS] for r in range(RES + 1)], axis=0)
    k_sin = jnp.concatenate([sin[r * per : r * per + STEPS] for r in range(RES + 1)], axis=0)
    kr[...] = rotate(k_flat, k_cos, k_sin).astype(BF16).astype(F32)

    def write_tokens(r, c, buf):
        both = values_new[r].astype(F32) if c else kr[pl.ds(r * STEPS, STEPS), :]
        block = 128

        def step(i, _):
            at = pl.ds(pl.multiple_of(i * block, block), block)
            place = lax.broadcasted_iota(jnp.int32, (block, HEAD), 0) + i * block - ctx[r]
            old = buf[at, :].astype(F32)
            buf[at, :] = jnp.where(place == 0, both[0:1], jnp.where(place == 1, both[1:2], old)).astype(BF16)
            return 0

        lax.fori_loop(0, WINDOW // block, step, 0)
        pltpu.make_async_copy(buf, (ko, vo)[c].at[r], o_sem.at[c, r]).start()

    def weigh(r, keys):
        q = qr[pl.ds(r * per, per), :].astype(BF16)
        s = lax.dot_general(q, keys[...], (((1,), (1,)), ((), ())), preferred_element_type=F32)
        s = s * (HEAD**-0.5)
        place = lax.broadcasted_iota(jnp.int32, s.shape, 1) - ctx[r]
        step = lax.rem(lax.broadcasted_iota(jnp.int32, s.shape, 0), STEPS)
        s = jnp.where(place <= step, s, -1e30)
        e = jnp.exp(s - jnp.max(s, axis=1, keepdims=True))
        p = (e / jnp.sum(e, axis=1, keepdims=True)).astype(BF16).astype(F32)
        prob[r] = jnp.where(place < 0, p, 0.0)
        for t in range(STEPS):
            fresh[t] = jnp.broadcast_to(jnp.sum(jnp.where(place == t, p, 0.0), axis=1, keepdims=True), fresh.shape[1:])

    def mix(r, values, at):
        o = jnp.dot(prob[r].astype(BF16), values[...], preferred_element_type=F32)
        both = values_new[r].astype(F32)
        for t in range(STEPS):
            o = o + fresh[t] * both[t : t + 1]
        for h in range(HEADS):
            mixed[pl.ds(at, STEPS), pl.ds(h * HEAD, HEAD)] = o[h * STEPS : (h + 1) * STEPS]

    share = attended.shape[2]

    def scatter(terms, sums, n, k):
        rows = mixed[...].astype(BF16)
        for i in (4, 3, 5, 2, 6, 1, 7, 0):
            to = lax.rem(tp + i, TP)
            cols = pl.ds(pl.multiple_of(to * share, 128), share)
            terms[to] = jnp.dot(rows, wv[:, cols], preferred_element_type=F32)[:n]
            if i == 0:
                continue
            pltpu.make_async_remote_copy(
                terms.at[to], sums.at[i], p_send.at[k], p_recv.at[k], device_id={"tp": to}, device_id_type=MESH
            ).start()
        sums[0] = terms[tp]

    mixed[...] = jnp.zeros_like(mixed)
    for r in range(RES):
        write_tokens(r, 0, res_k.at[r])
        weigh(r, res_k.at[r])
        mix(r, res_v.at[r], r * STEPS)
        write_tokens(r, 1, res_v.at[r])

    wait_bytes(r_sem.at[0, 0], spread_k.at[pl.ds(1, INST - 1)])
    send_second(0)
    loads[8].wait()
    scatter(part, got, RES * STEPS, 0)
    wait_bytes(r_sem.at[0, 1], spread_v.at[pl.ds(1, INST - 1)])
    send_second(1)
    others = pl.ds(1, TP - 1)
    wait_bytes(p_recv.at[0], got.at[others])
    total = jnp.sum(got[...], axis=0)
    for r in range(RES):
        attended[r] = total[r * STEPS : (r + 1) * STEPS].astype(attended.dtype)

    wait_bytes(r_sem.at[1, 0], arr.at[0, sent])
    write_tokens(RES, 0, arr.at[0])
    weigh(RES, arr.at[0])
    for c in range(2):
        wait_bytes(s_sem.at[0, c], arr.at[c, sent])
    wait_bytes(s_sem.at[1, 0], arr.at[0, sent])
    for c in range(2):
        for r in range(RES + 1 - c):
            pltpu.make_async_copy(res_k.at[0], (ko, vo)[c].at[r], o_sem.at[c, r]).wait()

    wait_bytes(r_sem.at[1, 1], arr.at[1, sent])
    mix(RES, arr.at[1], 0)
    scatter(part_l, got_l, STEPS, 1)
    write_tokens(RES, 1, arr.at[1])
    wait_bytes(p_send.at[0], part.at[others])
    wait_bytes(p_recv.at[1], got_l.at[others])
    attended[RES] = jnp.sum(got_l[...], axis=0).astype(attended.dtype)
    pltpu.make_async_copy(arr.at[1], vo.at[RES], o_sem.at[1, RES]).wait()
    wait_bytes(s_sem.at[1, 1], arr.at[1, sent])
    wait_bytes(p_send.at[1], part_l.at[others])


def put(*refs):
    n = len(refs) // 2
    copies = [pltpu.make_async_copy(refs[i], refs[n + i], refs[-1].at[i]) for i in range(n)]
    for copy in copies:
        copy.start()
    for copy in copies:
        copy.wait()


def local(queries, keys_new, values_new, key_cache, value_cache, lengths, migration, out_weight):
    rows = queries.shape[0]
    share = out_weight.shape[1] // TP
    hbm, vmem, anywhere = (pl.BlockSpec(memory_space=m) for m in (pltpu.HBM, pltpu.VMEM, pl.ANY))
    cache = (WINDOW, HEAD)
    n_q = rows * HEADS * STEPS
    migration = migration.T
    shapes = [((rows, STEPS, share), BF16), ((rows, *cache), BF16), ((rows, *cache), BF16)]
    outs = pl.pallas_call(
        kernel,
        out_shape=[pltpu.VMEM(*s) for s in shapes],
        in_specs=[hbm] * 8,
        out_specs=[vmem, anywhere, anywhere],
        scratch_shapes=[
            pltpu.SMEM(lengths.shape, jnp.int32),
            pltpu.SMEM(migration.shape, jnp.int32),
            pltpu.VMEM(migration.shape, jnp.int32),
            pltpu.VMEM(queries.shape, BF16),
            pltpu.VMEM(keys_new.shape, BF16),
            pltpu.VMEM(values_new.shape, BF16),
            pltpu.VMEM((RES, *cache), BF16),
            pltpu.VMEM((RES, *cache), BF16),
            pltpu.VMEM((2, *cache), BF16),
            pltpu.VMEM((2, *cache), BF16),
            pltpu.VMEM((INST, PIECE, HEAD), BF16),
            pltpu.VMEM((INST, PIECE, HEAD), BF16),
            pltpu.VMEM((2, *cache), BF16),
            pltpu.VMEM(out_weight.shape, BF16),
            pltpu.VMEM((INST, 128), jnp.int32),
            pltpu.SMEM((INST, 128), jnp.int32),
            pltpu.VMEM((n_q, HEAD), F32),
            pltpu.VMEM((rows * STEPS, HEAD), F32),
            pltpu.VMEM((rows, HEADS * STEPS, WINDOW), F32),
            pltpu.VMEM((STEPS, HEADS * STEPS, HEAD), F32),
            pltpu.VMEM((8, HEADS * HEAD), F32),
            pltpu.VMEM((TP, RES * STEPS, share), F32),
            pltpu.VMEM((TP, RES * STEPS, share), F32),
            pltpu.VMEM((TP, STEPS, share), F32),
            pltpu.VMEM((TP, STEPS, share), F32),
            pltpu.SemaphoreType.DMA((9,)),
            pltpu.SemaphoreType.DMA,
            pltpu.SemaphoreType.DMA((2, 2)),
            pltpu.SemaphoreType.DMA((2, 2)),
            pltpu.SemaphoreType.DMA((2, rows)),
            pltpu.SemaphoreType.DMA((2,)),
            pltpu.SemaphoreType.DMA((2,)),
        ],
        compiler_params=pltpu.CompilerParams(
            collective_id=0, has_side_effects=True, vmem_limit_bytes=24 << 20
        ),
        cost_estimate=pl.CostEstimate(flops=50_000_000, bytes_accessed=8 << 20, transcendentals=40_000),
    )(*(
        pltpu.with_memory_space_constraint(v, pltpu.HBM)
        for v in (lengths, migration, queries, keys_new, values_new, key_cache, value_cache, out_weight)
    ))
    return pl.pallas_call(
        put,
        out_shape=[jax.ShapeDtypeStruct(*s) for s in shapes],
        in_specs=[anywhere] * 3,
        out_specs=[anywhere] * 3,
        scratch_shapes=[pltpu.SemaphoreType.DMA((3,))],
        compiler_params=pltpu.CompilerParams(vmem_limit_bytes=1 << 20),
        cost_estimate=pl.CostEstimate(flops=0, bytes_accessed=4 << 20, transcendentals=0),
    )(*(pltpu.with_memory_space_constraint(v, pltpu.VMEM) for v in outs))


def solution(mesh):
    in_specs = (
        P("inst", None, "tp"),
        P("inst", None, "tp"),
        P("inst", None, "tp"),
        P("inst", None, "tp"),
        P("inst", None, "tp"),
        P(),
        P(),
        P("tp", None),
    )
    out_specs = (P("inst", None, "tp"), P("inst", None, "tp"), P("inst", None, "tp"))
    return jax.shard_map(local, mesh=mesh, in_specs=in_specs, out_specs=out_specs, check_vma=False)
```
